768 devices in a mesh: replica: 6 (over z_hi, core), dp: 128 (over y, x, z_lo).
Axes of the slice: x: 4, y: 8, z: 12 (z_hi: 3, z_lo: 4; z = z_hi * 4 + z_lo), core: 2. Of those that a mesh axis runs over, the one named last changes fastest.
Arguments:
- layer_input: bfloat16 [6, 49152, 3072], P('replica', 'dp'), may hold values from -24 to 24
- key_cotangent: bfloat16 [6, 49152, 512], P('replica', 'dp'), may hold values from -0.029907227 to 0.029907227
- local_params: float32 [6, 3072, 512], P('replica', 'dp'), may hold values from -6 to 6
- global_params: float32 [3072, 512], P('dp'), may hold values from -6 to 6
- outer_momentum: float32 [128, 24, 512], P('dp', 'replica'), may hold values from -3 to 3
- adam_first: float32 [6, 3072, 512], P('replica', 'dp'), may hold values from -2 to 2
- adam_second: float32 [6, 3072, 512], P('replica', 'dp'), may hold values from 0.25 to 4
Outputs:
- merged_params: bfloat16 [6, 3072, 512], P('replica')
- new_global: float32 [3072, 512], P('dp')
- new_momentum: float32 [128, 24, 512], P('dp', 'replica')
- new_first: float32 [6, 3072, 512], P('replica', 'dp')
- new_second: float32 [6, 3072, 512], P('replica', 'dp')
The draws below stay inside these ranges and needn't reach their ends.
All inputs are finite; a program needn't handle non-finite values.
Results may differ from the reference program's by a relative error of at most 0.0004.
Values may be sent and summed in bfloat16 or wider, within the bound.
No kernel may reach another device: no remote copies, remote signals or barrier semaphores. Data moves between devices by JAX's collectives and lax.ppermute only.
A program may use at most 32 MiB of HBM per device.

```python
import math
import jax
import jax.numpy as jnp
from jax import lax

DW = 3072
KW = 512
TOKENS = 49152
N_REPLICA = 6
N_DP = 128


def spiked(values, own_key, source, target, shards_of, factor):
    owner, partner = [(jnp.arange(values.shape[axis_at]) // (values.shape[axis_at] // shards_of)).reshape([-1 if axis == axis_at else 1 for axis in range(values.ndim)]) for axis_at in (source, target)]
    chosen = jax.random.permutation(own_key, shards_of)[partner]
    strong = (owner == chosen) | (owner == (partner + shards_of // 2) % shards_of)
    return jnp.where(strong, factor * values, values)


def shard_levels(stream_key, dims, shards, low, largest):
    def one(position, shards_of):
        steps = jax.random.uniform(jax.random.fold_in(jax.random.fold_in(stream_key, 6), position), (shards_of,), jnp.float32, low / len(shards), largest / len(shards))
        return jnp.repeat(jnp.exp(steps), dims[position] // shards_of).reshape((-1,) + (1,) * (len(dims) - position - 1))

    loudness = one(*shards[0])
    for cut in shards[1:]:
        loudness = loudness * one(*cut)
    return loudness


def centred(stream_key, dims, scale, most, split=(), kind=jnp.bfloat16):
    values = jax.random.normal(stream_key, dims, jnp.float32) * scale
    if len(split) > 0:
        values = shard_levels(stream_key, dims, split, -0.22, 0.18) * values
    return jnp.clip(values, min=-most, max=most).astype(kind)


def gaussian_with(rng, extent, scale, limit, shards, heavy, kind=jnp.bfloat16):
    result = scale * jax.random.normal(rng, extent, jnp.float32)
    if shards:
        result = result * shard_levels(rng, extent, shards, -0.22, 0.18)
    return jnp.clip(spiked(result, jax.random.fold_in(rng, 3), *heavy), -limit, limit).astype(kind)


def setup_inputs(seed: int = 0) -> dict:
    splits = jax.random.split(jax.random.key(seed), 8)
    layer_input = gaussian_with(splits[0], (N_REPLICA, TOKENS, DW), 1.0, 24.0, ((0, 6), (1, 128)), (1, 2, 128, 5.5))
    key_cotangent = centred(splits[1], (N_REPLICA, TOKENS, KW), 0.005, 0.029907227, ((0, 6), (1, 128)))
    local_params = centred(splits[2], (N_REPLICA, DW, KW), 1.0, 6.0, ((0, 6), (1, 128)), jnp.float32)
    global_params = centred(splits[3], (DW, KW), 1.0, 6.0, ((0, 128),), jnp.float32)
    outer_momentum = centred(splits[4], (N_DP, DW // N_DP, KW), 0.5, 3.0, ((0, 128), (1, 6)), jnp.float32)
    adam_first = centred(splits[5], (N_REPLICA, DW, KW), 0.3, 2.0, ((0, 6), (1, 128)), jnp.float32)
    adam_second = jnp.clip(jnp.exp(math.log(4.0) - 2.7725887 * jax.random.uniform(splits[6], (N_REPLICA, DW, KW), jnp.float32) ** shard_levels(splits[6], (N_REPLICA, DW, KW), ((0, 6), (1, 128)), -0.2, 0.2)), 0.25, 4.0)
    return {"layer_input": layer_input, "key_cotangent": key_cotangent, "local_params": local_params, "global_params": global_params, "outer_momentum": outer_momentum, "adam_first": adam_first, "adam_second": adam_second}


outer_mu = 0.9
outer_rate = 0.7
beta_one = 0.9
beta_two = 0.95
adam_eps = 1e-08
weight_decay = 0.1
inner_rate = 0.1
correct_one = 1.0 - 0.9 ** 50
correct_two = 1.0 - 0.95 ** 50

def reference(layer_input, key_cotangent, local_params, global_params, outer_momentum, adam_first, adam_second):
    gradients = []
    for replica_index in range(N_REPLICA):
        gradients.append(lax.dot_general(layer_input[replica_index], key_cotangent[replica_index], (((0,), (0,)), ((), ())), preferred_element_type=jnp.float32))
    gradient = jnp.stack(gradients)
    outer_grad = lax.optimization_barrier(jnp.mean(global_params[None] - local_params, axis=0))
    momentum_flat = outer_mu * outer_momentum.reshape(DW, KW) + outer_grad
    new_global = global_params - outer_rate * (outer_grad + outer_mu * momentum_flat)
    new_first = beta_one * adam_first + (1.0 - beta_one) * gradient
    new_second = beta_two * adam_second + (1.0 - beta_two) * gradient * gradient
    adam_step = new_first / correct_one / (jnp.sqrt(new_second / correct_two) + adam_eps) + weight_decay * local_params
    merged_params = (new_global[None] - inner_rate * adam_step).astype(jnp.bfloat16)
    new_momentum = momentum_flat.reshape(N_DP, DW // N_DP, KW)
    return (merged_params, new_global, new_momentum, new_first, new_second)
```

```python
import jax
import jax.numpy as jnp
from jax import lax
from jax.sharding import Mesh
from jax.sharding import PartitionSpec as P

DP = ("dp_0", "dp_1", "dp_2")
YZ = ("dp_0", "dp_2")

outer_mu = 0.9
outer_rate = 0.7
beta_one = 0.9
beta_two = 0.95
adam_eps = 1e-08
weight_decay = 0.1
inner_rate = 0.1
correct_one = 1.0 - 0.9**50
correct_two = 1.0 - 0.95**50


def exchanged(x, axes):
    return lax.all_to_all(x, axes, 0, 0, tiled=True)


def per_device(
    layer_input, key_cotangent, local_params, global_params, outer_momentum, adam_first, adam_second
):
    features = layer_input[0]
    cotangent = key_cotangent[0]
    own_local = local_params[0]
    rows, width = global_params.shape
    ny, nx, nz = (lax.axis_size(a) for a in DP)
    replicas = lax.axis_size("replica")
    deltas = global_params - own_local
    sub_rows = outer_momentum.shape[1]
    row_offset = lax.axis_index("replica") * sub_rows
    placed = lax.dynamic_update_slice_in_dim(
        jnp.zeros((rows, width), jnp.float32), outer_momentum[0], row_offset, 0
    )
    both = lax.psum(jnp.concatenate([deltas, placed], 0), "replica")
    outer_grad = both[:rows] / replicas
    momentum_all = outer_mu * both[rows:] + outer_grad
    global_new = global_params - outer_rate * (outer_grad + outer_mu * momentum_all)
    momentum_new = lax.dynamic_slice_in_dim(momentum_all, row_offset, sub_rows, 0)

    term = lax.dot_general(
        features, cotangent, (((0,), (0,)), ((), ())), preferred_element_type=jnp.float32
    ).astype(jnp.float16)
    term = term.reshape(ny, nx, nz * rows, width).transpose(1, 0, 2, 3)
    part = exchanged(term, "dp_1").astype(jnp.float32).sum(0).astype(jnp.float16)
    part = part.reshape(ny * nz, rows, width)
    gradient = exchanged(part, YZ).astype(jnp.float32).sum(0)

    first_new = beta_one * adam_first[0] + (1.0 - beta_one) * gradient
    second_new = beta_two * adam_second[0] + (1.0 - beta_two) * gradient * gradient
    adam_step = (
        first_new / correct_one / (jnp.sqrt(second_new / correct_two) + adam_eps)
        + weight_decay * own_local
    )
    merged = (global_new - inner_rate * adam_step).astype(jnp.bfloat16)
    plane = exchanged(jnp.broadcast_to(merged[None], (ny * nz, rows, width)), YZ)
    cube = exchanged(jnp.broadcast_to(plane[None], (nx, *plane.shape)), "dp_1")
    cube = cube.reshape(nx, ny, nz * rows, width).transpose(1, 0, 2, 3)
    gathered = cube.reshape(-1, width)
    return (gathered[None], global_new, momentum_new[None], first_new[None], second_new[None])


def solution(mesh):
    torus = Mesh(
        mesh.devices.reshape(mesh.shape["replica"], 8, 4, 4), ("replica", "dp_0", "dp_1", "dp_2")
    )
    in_specs = (
        P("replica", DP, None),
        P("replica", DP, None),
        P("replica", DP, None),
        P(DP, None),
        P(DP, "replica", None),
        P("replica", DP, None),
        P("replica", DP, None),
    )
    out_specs = (
        P("replica", None, None),
        P(DP, None),
        P(DP, "replica", None),
        P("replica", DP, None),
        P("replica", DP, None),
    )
    return jax.shard_map(
        per_device, mesh=torus, in_specs=in_specs, out_specs=out_specs, check_vma=False
    )
```

```python
import jax
import jax.numpy as jnp
from jax import lax
from jax.experimental import pallas as pl
from jax.experimental.pallas import tpu as pltpu
from jax.sharding import Mesh
from jax.sharding import PartitionSpec as P

DP = ("dp_0", "dp_1", "dp_2")
YZ = ("dp_0", "dp_2")
X = "dp_1"
HI, CORE = REPLICA = ("chip", "core")

outer_mu = 0.9
outer_rate = 0.7
beta_one = 0.9
beta_two = 0.95
adam_eps = 1e-08
weight_decay = 0.1
inner_rate = 0.1
correct_one = 1.0 - 0.9**50
correct_two = 1.0 - 0.95**50


def exchanged(x, axes):
    return lax.all_to_all(x, axes, 0, 0, tiled=True)


def copies(x, n):
    return jnp.broadcast_to(x[None], (n, *x.shape))


def total(blocks):
    parts = [b.astype(jnp.float32) for b in blocks]
    while len(parts) > 1:
        parts = [sum(parts[i : i + 2]) for i in range(0, len(parts), 2)]
    return parts[0]


def passed(x, axis, step):
    n = lax.axis_size(axis)
    return lax.ppermute(x, axis, [(i, (i + step) % n) for i in range(n)])


def turned(index, n):
    return index & (n - 1) if n & (n - 1) == 0 else lax.rem(index, n)


def block_of(x, index, dim):
    return lax.dynamic_index_in_dim(x, index, dim, keepdims=False)


def terms_along(x, axis, dim):
    n = lax.axis_size(axis)
    me = lax.axis_index(axis)
    mine = [block_of(x, turned(me + k, n), dim) for k in range(n)]
    return mine[:1] + [passed(mine[k], axis, k) for k in range(1, n)]


def arrived_along(x, axis):
    return [x] + [passed(x, axis, k) for k in range(1, lax.axis_size(axis))]


def placed_along(x, axis):
    n = lax.axis_size(axis)
    me = lax.axis_index(axis)
    blocks = jnp.stack(arrived_along(x, axis))
    return jnp.stack([block_of(blocks, turned(me + n - i, n), 0) for i in range(n)])


def joining(me_ref, *refs):
    *near, far, out = refs
    places = len(near)
    for k, ref in enumerate(near):
        x = turned(me_ref[0] + places - k, places)
        both = jnp.concatenate(
            [ref[0].astype(jnp.float32), far[0, :, x].astype(jnp.float32)], axis=1
        )
        piece = both.reshape(-1, both.shape[-1]).astype(out.dtype)
        start = pl.multiple_of(x * piece.shape[0], piece.shape[0])
        out[pl.ds(start, piece.shape[0]), :] = piece


def joined(near, far, me):
    ny, nz, cut, width = near[0].shape
    nx, rest = far.shape[2:4]
    block = nx * nz * (cut + rest)
    return pl.pallas_call(
        joining,
        grid_spec=pltpu.PrefetchScalarGridSpec(
            num_scalar_prefetch=1,
            grid=(ny,),
            in_specs=[pl.BlockSpec((1, nz, cut, width), lambda y, m: (y, 0, 0, 0))] * nx
            + [pl.BlockSpec((1, nz, nx, rest, width), lambda y, m: (y, 0, 0, 0, 0))],
            out_specs=pl.BlockSpec((block, width), lambda y, m: (y, 0)),
        ),
        out_shape=jax.ShapeDtypeStruct((ny * block, width), far.dtype),
        compiler_params=pltpu.CompilerParams(vmem_limit_bytes=16 * 2**20),
        name="joined",
    )(me.reshape(1), *near, far)


def per_device(
    layer_input, key_cotangent, local_params, global_params, outer_momentum, adam_first, adam_second
):
    features = layer_input[0]
    cotangent = key_cotangent[0]
    own_local = local_params[0]
    rows, width = global_params.shape
    ny, nx, nz = (lax.axis_size(a) for a in DP)
    plane = ny * nz
    n_hi, n_core = lax.axis_size(HI), lax.axis_size(CORE)
    replicas = n_hi * n_core
    sub_rows = outer_momentum.shape[1]
    cut = rows * 2 // 3

    core = lax.axis_index(CORE)
    hi = lax.axis_index(HI)
    deltas = global_params - own_local
    mine = jnp.concatenate([deltas, outer_momentum[0]], 0)
    other = passed(mine, CORE, 1)
    first, second = jnp.where(core == 0, mine, other), jnp.where(core == 0, other, mine)
    pair = jnp.concatenate([mine[:rows] + other[:rows], first[rows:], second[rows:]], 0)
    by_chip = placed_along(pair, HI)
    outer_grad = sum(p[:rows] for p in by_chip) / replicas
    old_rows = jnp.concatenate([p[rows:] for p in by_chip], 0)
    momentum_all = outer_mu * old_rows + outer_grad
    global_new = global_params - outer_rate * (outer_grad + outer_mu * momentum_all)
    momentum_new = lax.dynamic_slice_in_dim(
        momentum_all, (hi * n_core + core) * sub_rows, sub_rows, 0
    )

    term = lax.dot_general(
        features, cotangent, (((0,), (0,)), ((), ())), preferred_element_type=jnp.float32
    ).astype(jnp.float16)
    term = term.reshape(ny, nx, nz, rows, width)
    term_b = term[:, :, :, cut:].transpose(0, 2, 1, 3, 4).reshape(plane, nx, rows - cut, width)
    got_a = terms_along(term[:, :, :, :cut], X, 1)
    got_b = exchanged(term_b, YZ)

    part_a, part_b = lax.optimization_barrier(
        (total(got_a).astype(jnp.float16).reshape(plane, cut, width), total(got_b).astype(jnp.float16))
    )
    sum_a = exchanged(part_a, YZ)
    sum_b = terms_along(part_b, X, 0)

    def stepped(gradient, lo, hi):
        first_new = beta_one * adam_first[0, lo:hi] + (1.0 - beta_one) * gradient
        second_new = beta_two * adam_second[0, lo:hi] + (1.0 - beta_two) * gradient * gradient
        adam_step = (
            first_new / correct_one / (jnp.sqrt(second_new / correct_two) + adam_eps)
            + weight_decay * own_local[lo:hi]
        )
        merged = (global_new[lo:hi] - inner_rate * adam_step).astype(jnp.bfloat16)
        return merged, first_new, second_new

    merged_a, first_a, second_a = stepped(total(sum_a), 0, cut)
    merged_b, first_b, second_b = stepped(total(sum_b), cut, rows)
    near_b = placed_along(merged_b, X)
    near_a, near_b = lax.optimization_barrier((exchanged(copies(merged_a, plane), YZ), near_b))
    all_a = [n.reshape(ny, nz, cut, width) for n in arrived_along(near_a, X)]
    all_b = exchanged(copies(near_b, plane), YZ).reshape(ny, nz, nx, rows - cut, width)
    gathered = joined(all_a, all_b, lax.axis_index(X))
    first_new = jnp.concatenate([first_a, first_b], 0)
    second_new = jnp.concatenate([second_a, second_b], 0)
    return (gathered[None], global_new, momentum_new[None], first_new[None], second_new[None])


def solution(mesh):
    torus = Mesh(
        mesh.devices.reshape(mesh.shape["replica"] // 2, 2, 8, 4, 4), REPLICA + DP
    )
    in_specs = (
        P(REPLICA, DP, None),
        P(REPLICA, DP, None),
        P(REPLICA, DP, None),
        P(DP, None),
        P(DP, REPLICA, None),
        P(REPLICA, DP, None),
        P(REPLICA, DP, None),
    )
    out_specs = (
        P(REPLICA, None, None),
        P(DP, None),
        P(DP, REPLICA, None),
        P(REPLICA, DP, None),
        P(REPLICA, DP, None),
    )
    return jax.shard_map(
        per_device, mesh=torus, in_specs=in_specs, out_specs=out_specs, check_vma=False
    )
```

```python
import jax
import jax.numpy as jnp
from jax import lax
from jax.experimental import pallas as pl
from jax.experimental.pallas import tpu as pltpu
from jax.sharding import Mesh
from jax.sharding import PartitionSpec as P

DP = ("dp_0", "dp_1", "dp_2")
YZ = ("dp_0", "dp_2")
X = "dp_1"
HI, CORE = REPLICA = ("chip", "core")

outer_mu = 0.9
outer_rate = 0.7
beta_one = 0.9
beta_two = 0.95
adam_eps = 1e-08
weight_decay = 0.1
inner_rate = 0.1
correct_one = 1.0 - 0.9**50
correct_two = 1.0 - 0.95**50


def exchanged(x, axes):
    return lax.all_to_all(x, axes, 0, 0, tiled=True)


def copies(x, n):
    return jnp.broadcast_to(x[None], (n, *x.shape))


def total(blocks):
    parts = [b.astype(jnp.float32) for b in blocks]
    while len(parts) > 1:
        parts = [sum(parts[i : i + 2]) for i in range(0, len(parts), 2)]
    return parts[0]


def passed(x, axis, step):
    n = lax.axis_size(axis)
    return lax.ppermute(x, axis, [(i, (i + step) % n) for i in range(n)])


def turned(index, n):
    return index & (n - 1) if n & (n - 1) == 0 else lax.rem(index, n)


def block_of(x, index, dim):
    return lax.dynamic_index_in_dim(x, index, dim, keepdims=False)


def terms_along(x, axis, dim, cut):
    n = lax.axis_size(axis)
    me = lax.axis_index(axis)
    sizes = list(x.shape)
    sizes[dim], sizes[-2] = 1, cut

    def block(index):
        starts = [0] * x.ndim
        starts[dim] = index
        return lax.dynamic_slice(x, starts, sizes)

    mine = [block(turned(me + k, n)) for k in range(n)]
    return mine[:1] + [passed(mine[k], axis, k) for k in range(1, n)]


def arrived_along(x, axis):
    return [x] + [passed(x, axis, k) for k in range(1, lax.axis_size(axis))]


def placed_along(x, axis):
    n = lax.axis_size(axis)
    me = lax.axis_index(axis)
    blocks = jnp.stack(arrived_along(x, axis))
    return jnp.stack([block_of(blocks, turned(me + n - i, n), 0) for i in range(n)])


def joining(me_ref, *refs):
    *near, far, out = refs
    places = len(near)
    for k, ref in enumerate(near):
        x = turned(me_ref[0] + places - k, places)
        for y in range(ref.shape[0]):
            both = jnp.concatenate(
                [ref[y].astype(jnp.float32), far[y, :, x].astype(jnp.float32)], axis=1
            )
            piece = both.reshape(-1, both.shape[-1]).astype(out.dtype)
            start = pl.multiple_of((x + y * places) * piece.shape[0], piece.shape[0])
            out[pl.ds(start, piece.shape[0]), :] = piece


def joined(near, far, me):
    ny, nz, cut, width = near[0].shape
    nx, rest = far.shape[2:4]
    step = 2
    block = step * nx * nz * (cut + rest)
    return pl.pallas_call(
        joining,
        grid_spec=pltpu.PrefetchScalarGridSpec(
            num_scalar_prefetch=1,
            grid=(ny // step,),
            in_specs=[pl.BlockSpec((step, nz, cut, width), lambda y, m: (y, 0, 0, 0))] * nx
            + [pl.BlockSpec((step, nz, nx, rest, width), lambda y, m: (y, 0, 0, 0, 0))],
            out_specs=pl.BlockSpec((block, width), lambda y, m: (y, 0)),
        ),
        out_shape=jax.ShapeDtypeStruct((ny // step * block, width), far.dtype),
        compiler_params=pltpu.CompilerParams(vmem_limit_bytes=24 * 2**20),
        name="joined",
    )(me.reshape(1), *near, far)


def per_device(
    layer_input, key_cotangent, local_params, global_params, outer_momentum, adam_first, adam_second
):
    features = layer_input[0]
    cotangent = key_cotangent[0]
    own_local = local_params[0]
    rows, width = global_params.shape
    ny, nx, nz = (lax.axis_size(a) for a in DP)
    plane = ny * nz
    n_hi, n_core = lax.axis_size(HI), lax.axis_size(CORE)
    replicas = n_hi * n_core
    sub_rows = outer_momentum.shape[1]
    cut = rows * 2 // 3

    core = lax.axis_index(CORE)
    hi = lax.axis_index(HI)
    deltas = global_params - own_local
    mine = jnp.concatenate([deltas, outer_momentum[0]], 0)
    other = passed(mine, CORE, 1)

    term = lax.dot_general(
        features, cotangent, (((0,), (0,)), ((), ())), preferred_element_type=jnp.float32
    ).astype(jnp.float16)
    term, other = lax.optimization_barrier((term, other))
    term = term.reshape(ny, nx, nz, rows, width)
    term_b = term[:, :, :, cut:].transpose(0, 2, 1, 3, 4).reshape(plane, nx, rows - cut, width)
    got_a = terms_along(term, X, 1, cut)
    got_b = exchanged(term_b, YZ)

    first, second = jnp.where(core == 0, mine, other), jnp.where(core == 0, other, mine)
    pair = jnp.concatenate([mine[:rows] + other[:rows], first[rows:], second[rows:]], 0)
    pair, got_a[1] = lax.optimization_barrier((pair, got_a[1]))
    by_chip = placed_along(pair, HI)
    outer_grad = sum(p[:rows] for p in by_chip) / replicas
    old_rows = jnp.concatenate([p[rows:] for p in by_chip], 0)
    momentum_all = outer_mu * old_rows + outer_grad
    global_new = global_params - outer_rate * (outer_grad + outer_mu * momentum_all)
    momentum_new = lax.dynamic_slice_in_dim(
        momentum_all, (hi * n_core + core) * sub_rows, sub_rows, 0
    )

    part_a = total(got_a).astype(jnp.float16).reshape(plane, cut, width)
    part_b = total(got_b).astype(jnp.float16)
    part_a, part_b, global_new, momentum_new = lax.optimization_barrier(
        (part_a, part_b, global_new, momentum_new)
    )
    sum_a = exchanged(part_a, YZ)
    sum_b = [t[0] for t in terms_along(part_b, X, 0, rows - cut)]

    def stepped(gradient, lo, hi):
        first_new = beta_one * adam_first[0, lo:hi] + (1.0 - beta_one) * gradient
        second_new = beta_two * adam_second[0, lo:hi] + (1.0 - beta_two) * gradient * gradient
        adam_step = (
            first_new / correct_one / (jnp.sqrt(second_new / correct_two) + adam_eps)
            + weight_decay * own_local[lo:hi]
        )
        merged = (global_new[lo:hi] - inner_rate * adam_step).astype(jnp.bfloat16)
        return merged, first_new, second_new

    merged_a, first_a, second_a = stepped(total(sum_a), 0, cut)
    merged_b, first_b, second_b = stepped(total(sum_b), cut, rows)
    merged_a, merged_b = lax.optimization_barrier((merged_a, merged_b))
    near_b = placed_along(merged_b, X)
    near_a, near_b = lax.optimization_barrier((exchanged(copies(merged_a, plane), YZ), near_b))
    all_a = [n.reshape(ny, nz, cut, width) for n in arrived_along(near_a, X)]
    all_b = exchanged(copies(near_b, plane), YZ).reshape(ny, nz, nx, rows - cut, width)
    gathered = joined(all_a, all_b, lax.axis_index(X))
    first_new = jnp.concatenate([first_a, first_b], 0)
    second_new = jnp.concatenate([second_a, second_b], 0)
    return (gathered[None], global_new, momentum_new[None], first_new[None], second_new[None])


def solution(mesh):
    torus = Mesh(
        mesh.devices.reshape(mesh.shape["replica"] // 2, 2, 8, 4, 4), REPLICA + DP
    )
    in_specs = (
        P(REPLICA, DP, None),
        P(REPLICA, DP, None),
        P(REPLICA, DP, None),
        P(DP, None),
        P(DP, REPLICA, None),
        P(REPLICA, DP, None),
        P(REPLICA, DP, None),
    )
    out_specs = (
        P(REPLICA, None, None),
        P(DP, None),
        P(DP, REPLICA, None),
        P(REPLICA, DP, None),
        P(REPLICA, DP, None),
    )
    return jax.shard_map(
        per_device, mesh=torus, in_specs=in_specs, out_specs=out_specs, check_vma=False
    )
```

```python
import jax
import jax.numpy as jnp
from jax import lax
from jax.experimental import pallas as pl
from jax.experimental.pallas import tpu as pltpu
from jax.sharding import Mesh
from jax.sharding import PartitionSpec as P

DP = ("dp_0", "dp_1", "dp_2")
YZ = ("dp_0", "dp_2")
X = "dp_1"
HI, CORE = REPLICA = ("chip", "core")

outer_mu = 0.9
outer_rate = 0.7
beta_one = 0.9
beta_two = 0.95
adam_eps = 1e-08
weight_decay = 0.1
inner_rate = 0.1
correct_one = 1.0 - 0.9**50
correct_two = 1.0 - 0.95**50


def exchanged(x, axes):
    return lax.all_to_all(x, axes, 0, 0, tiled=True)


def copies(x, n):
    return jnp.broadcast_to(x[None], (n, *x.shape))


def total(blocks):
    parts = [b.astype(jnp.float32) for b in blocks]
    while len(parts) > 1:
        parts = [sum(parts[i : i + 2]) for i in range(0, len(parts), 2)]
    return parts[0]


def passed(x, axis, step):
    n = lax.axis_size(axis)
    return lax.ppermute(x, axis, [(i, (i + step) % n) for i in range(n)])


def turned(index, n):
    return index & (n - 1) if n & (n - 1) == 0 else lax.rem(index, n)


def block_of(x, index, dim):
    return lax.dynamic_index_in_dim(x, index, dim, keepdims=False)


def blocks_along(x, axis, dim):
    n = lax.axis_size(axis)
    me = lax.axis_index(axis)
    return [block_of(x, turned(me + k, n), dim) for k in range(n)]


def terms_along(blocks, axis):
    return blocks[:1] + [passed(blocks[k], axis, k) for k in range(1, len(blocks))]


def arrived_along(x, axis):
    return [x] + [passed(x, axis, k) for k in range(1, lax.axis_size(axis))]


def placed_along(x, axis):
    n = lax.axis_size(axis)
    me = lax.axis_index(axis)
    blocks = jnp.stack(arrived_along(x, axis))
    return jnp.stack([block_of(blocks, turned(me + n - i, n), 0) for i in range(n)])


def joining(me_ref, *refs):
    *near, far, out, near_in, far_in, held, got, sent = refs
    places = len(near)
    ny = far.shape[0]
    me = me_ref[0]

    def loads(y):
        return [
            pltpu.make_async_copy(ref.at[y], near_in.at[k, y], got.at[k, y])
            for k, ref in enumerate(near)
        ] + [pltpu.make_async_copy(far.at[y], far_in.at[y], got.at[places, y])]

    def store(y):
        return pltpu.make_async_copy(held.at[y], out.at[y], sent.at[y])

    for y in range(ny):
        for copy in loads(y):
            copy.start()
    for y in range(ny):
        for copy in loads(y):
            copy.wait()
        for k in range(places):
            x = turned(me + places - k, places)
            both = jnp.concatenate(
                [near_in[k, y].astype(jnp.float32), far_in[y, :, x].astype(jnp.float32)], axis=1
            )
            held[y, x] = both.reshape(-1, both.shape[-1]).astype(out.dtype)
        store(y).start()
    for y in range(ny):
        store(y).wait()


def joined(near, far, me):
    ny, nz, cut, width = near[0].shape
    nx, rest = far.shape[2:4]
    shape = (ny, nx, nz * (cut + rest), width)
    place = pl.BlockSpec(memory_space=pl.ANY)
    out = pl.pallas_call(
        joining,
        in_specs=[pl.BlockSpec(memory_space=pltpu.SMEM)] + [place] * (nx + 1),
        out_specs=place,
        out_shape=jax.ShapeDtypeStruct(shape, far.dtype),
        scratch_shapes=[
            pltpu.VMEM((nx, *near[0].shape), far.dtype),
            pltpu.VMEM(far.shape, far.dtype),
            pltpu.VMEM(shape, far.dtype),
            pltpu.SemaphoreType.DMA((nx + 1, ny)),
            pltpu.SemaphoreType.DMA((ny,)),
        ],
        name="joined",
    )(me.reshape(1), *near, far)
    return out.reshape(-1, width)


def per_device(
    layer_input, key_cotangent, local_params, global_params, outer_momentum, adam_first, adam_second
):
    features = layer_input[0]
    cotangent = key_cotangent[0]
    own_local = local_params[0]
    rows, width = global_params.shape
    ny, nx, nz = (lax.axis_size(a) for a in DP)
    plane = ny * nz
    n_hi, n_core = lax.axis_size(HI), lax.axis_size(CORE)
    replicas = n_hi * n_core
    sub_rows = outer_momentum.shape[1]
    cut = rows * 2 // 3

    core = lax.axis_index(CORE)
    hi = lax.axis_index(HI)
    deltas = global_params - own_local
    mine = jnp.concatenate([deltas, outer_momentum[0]], 0)
    other = passed(mine, CORE, 1)

    half = width // 2

    def product(columns):
        return lax.dot_general(
            features, columns, (((0,), (0,)), ((), ())), preferred_element_type=jnp.float32
        ).astype(jnp.float16)

    term_b = product(cotangent[:, half:]).reshape(ny, nx, nz, rows, half)
    got_b = exchanged(term_b.transpose(0, 2, 1, 3, 4).reshape(plane, nx, rows, half), YZ)
    term_a = product(cotangent[:, :half]).reshape(ny, nx, nz * rows, half)
    got_a = terms_along(blocks_along(term_a, X, 1), X)

    first, second = jnp.where(core == 0, mine, other), jnp.where(core == 0, other, mine)
    pair = jnp.concatenate([mine[:rows] + other[:rows], first[rows:], second[rows:]], 0)
    pair, got_a[1], got_a[3] = lax.optimization_barrier((pair, got_a[1], got_a[3]))
    by_chip = placed_along(pair, HI)
    outer_grad = sum(p[:rows] for p in by_chip) / replicas
    old_rows = jnp.concatenate([p[rows:] for p in by_chip], 0)
    momentum_all = outer_mu * old_rows + outer_grad
    global_new = global_params - outer_rate * (outer_grad + outer_mu * momentum_all)
    momentum_new = lax.dynamic_slice_in_dim(
        momentum_all, (hi * n_core + core) * sub_rows, sub_rows, 0
    )

    part_a = total(got_a).astype(jnp.float16).reshape(plane, rows, half)
    part_b = total(got_b).astype(jnp.float16)
    part_a, part_b, global_new, momentum_new = lax.optimization_barrier(
        (part_a, part_b, global_new, momentum_new)
    )
    sum_a = exchanged(part_a, YZ)
    sum_b = terms_along(blocks_along(part_b, X, 0), X)
    gradient = jnp.concatenate([total(sum_a), total(sum_b)], 1)

    first_new = beta_one * adam_first[0] + (1.0 - beta_one) * gradient
    second_new = beta_two * adam_second[0] + (1.0 - beta_two) * gradient * gradient
    adam_step = (
        first_new / correct_one / (jnp.sqrt(second_new / correct_two) + adam_eps)
        + weight_decay * own_local
    )
    merged = (global_new - inner_rate * adam_step).astype(jnp.bfloat16)
    merged_a, merged_b = merged[:cut], merged[cut:]
    near_b = placed_along(merged_b, X)
    near_a, near_b = lax.optimization_barrier((exchanged(copies(merged_a, plane), YZ), near_b))
    all_a = [n.reshape(ny, nz, cut, width) for n in arrived_along(near_a, X)]
    all_b = exchanged(copies(near_b, plane), YZ).reshape(ny, nz, nx, rows - cut, width)
    gathered = joined(all_a, all_b, lax.axis_index(X))
    return (gathered[None], global_new, momentum_new[None], first_new[None], second_new[None])


def solution(mesh):
    torus = Mesh(
        mesh.devices.reshape(mesh.shape["replica"] // 2, 2, 8, 4, 4), REPLICA + DP
    )
    in_specs = (
        P(REPLICA, DP, None),
        P(REPLICA, DP, None),
        P(REPLICA, DP, None),
        P(DP, None),
        P(DP, REPLICA, None),
        P(REPLICA, DP, None),
        P(REPLICA, DP, None),
    )
    out_specs = (
        P(REPLICA, None, None),
        P(DP, None),
        P(DP, REPLICA, None),
        P(REPLICA, DP, None),
        P(REPLICA, DP, None),
    )
    return jax.shard_map(
        per_device, mesh=torus, in_specs=in_specs, out_specs=out_specs, check_vma=False
    )
```

```python
import jax
import jax.numpy as jnp
from jax import lax
from jax.experimental import pallas as pl
from jax.experimental.pallas import tpu as pltpu
from jax.sharding import Mesh
from jax.sharding import PartitionSpec as P

DP = ("dp_0", "dp_1", "dp_2")
YZ = ("dp_0", "dp_2")
X = "dp_1"
HI, CORE = REPLICA = ("chip", "core")

outer_mu = 0.9
outer_rate = 0.7
beta_one = 0.9
beta_two = 0.95
adam_eps = 1e-08
weight_decay = 0.1
inner_rate = 0.1
correct_one = 1.0 - 0.9**50
correct_two = 1.0 - 0.95**50


def exchanged(x, axes):
    return lax.all_to_all(x, axes, 0, 0, tiled=True)


def copies(x, n):
    return jnp.broadcast_to(x[None], (n, *x.shape))


def total(blocks):
    parts = [b.astype(jnp.float32) for b in blocks]
    while len(parts) > 1:
        parts = [sum(parts[i : i + 2]) for i in range(0, len(parts), 2)]
    return parts[0]


def passed(x, axis, step):
    n = lax.axis_size(axis)
    return lax.ppermute(x, axis, [(i, (i + step) % n) for i in range(n)])


def turned(index, n):
    return index & (n - 1) if n & (n - 1) == 0 else lax.rem(index, n)


def block_of(x, index, dim):
    return lax.dynamic_index_in_dim(x, index, dim, keepdims=False)


def blocks_along(x, axis, dim):
    n = lax.axis_size(axis)
    me = lax.axis_index(axis)
    return [block_of(x, turned(me + k, n), dim) for k in range(n)]


def terms_along(blocks, axis):
    return blocks[:1] + [passed(blocks[k], axis, k) for k in range(1, len(blocks))]


def arrived_along(x, axis):
    return [x] + [passed(x, axis, k) for k in range(1, lax.axis_size(axis))]


def in_order(arrived, axis):
    n = lax.axis_size(axis)
    me = lax.axis_index(axis)
    blocks = jnp.stack(arrived)
    return jnp.stack([block_of(blocks, turned(me + n - i, n), 0) for i in range(n)])


def placed_along(x, axis):
    return in_order(arrived_along(x, axis), axis)


def joining(me_ref, *refs):
    *near, far, out, near_in, far_in, held, got, sent = refs
    places = len(near)
    ny = far.shape[0]
    me = me_ref[0]

    def loads(y):
        return [
            pltpu.make_async_copy(ref.at[y], near_in.at[k, y], got.at[k, y])
            for k, ref in enumerate(near)
        ] + [pltpu.make_async_copy(far.at[y], far_in.at[y], got.at[places, y])]

    def store(y):
        return pltpu.make_async_copy(held.at[y], out.at[y], sent.at[y])

    for y in range(ny):
        for copy in loads(y):
            copy.start()
    for y in range(ny):
        for copy in loads(y):
            copy.wait()
        for k in range(places):
            x = turned(me + places - k, places)
            both = jnp.concatenate(
                [near_in[k, y].astype(jnp.float32), far_in[y, :, x].astype(jnp.float32)], axis=1
            )
            held[y, x] = both.reshape(-1, both.shape[-1]).astype(out.dtype)
        store(y).start()
    for y in range(ny):
        store(y).wait()


def joined(near, far, me):
    ny, nz, cut, width = near[0].shape
    nx, rest = far.shape[2:4]
    shape = (ny, nx, nz * (cut + rest), width)
    place = pl.BlockSpec(memory_space=pl.ANY)
    out = pl.pallas_call(
        joining,
        in_specs=[pl.BlockSpec(memory_space=pltpu.SMEM)] + [place] * (nx + 1),
        out_specs=place,
        out_shape=jax.ShapeDtypeStruct(shape, far.dtype),
        scratch_shapes=[
            pltpu.VMEM((nx, *near[0].shape), far.dtype),
            pltpu.VMEM(far.shape, far.dtype),
            pltpu.VMEM(shape, far.dtype),
            pltpu.SemaphoreType.DMA((nx + 1, ny)),
            pltpu.SemaphoreType.DMA((ny,)),
        ],
        name="joined",
    )(me.reshape(1), *near, far)
    return out.reshape(-1, width)


def per_device(
    layer_input, key_cotangent, local_params, global_params, outer_momentum, adam_first, adam_second
):
    features = layer_input[0]
    cotangent = key_cotangent[0]
    own_local = local_params[0]
    rows, width = global_params.shape
    ny, nx, nz = (lax.axis_size(a) for a in DP)
    plane = ny * nz
    n_hi, n_core = lax.axis_size(HI), lax.axis_size(CORE)
    replicas = n_hi * n_core
    sub_rows = outer_momentum.shape[1]
    cut = rows * 2 // 3

    core = lax.axis_index(CORE)
    hi = lax.axis_index(HI)
    mine = jnp.concatenate([own_local, outer_momentum[0]], 0)
    chips = arrived_along(mine, HI)

    half = width // 2

    def product(columns):
        return lax.dot_general(
            features, columns, (((0,), (0,)), ((), ())), preferred_element_type=jnp.float32
        ).astype(jnp.float16)

    term_b = product(cotangent[:, half:]).reshape(ny, nx, nz, rows, half)
    term_b = term_b.transpose(0, 2, 1, 3, 4).reshape(plane, nx, rows, half)
    term_b, chips = lax.optimization_barrier((term_b, chips))
    got_b = exchanged(term_b, YZ)
    term_a = product(cotangent[:, :half]).reshape(ny, nx, nz * rows, half)
    got_a = terms_along(blocks_along(term_a, X, 1), X)

    chips, got_a[1] = lax.optimization_barrier((chips, got_a[1]))
    by_chip = in_order(chips, HI)
    summed = jnp.concatenate(
        [sum(global_params - c[:rows] for c in by_chip)] + [c[rows:] for c in by_chip], 0
    )
    other = passed(summed, CORE, 1)
    outer_grad = (summed[:rows] + other[:rows]) / replicas
    by_core = jnp.where(core == 0, jnp.stack([summed, other]), jnp.stack([other, summed]))
    old_rows = by_core[:, rows:].reshape(n_core, n_hi, sub_rows, width)
    old_rows = old_rows.transpose(1, 0, 2, 3).reshape(rows, width)
    momentum_all = outer_mu * old_rows + outer_grad
    global_new = global_params - outer_rate * (outer_grad + outer_mu * momentum_all)
    momentum_new = lax.dynamic_slice_in_dim(
        momentum_all, (hi * n_core + core) * sub_rows, sub_rows, 0
    )

    part_a = total(got_a).astype(jnp.float16).reshape(plane, rows, half)
    part_b = total(got_b).astype(jnp.float16)
    part_a, part_b, global_new, momentum_new = lax.optimization_barrier(
        (part_a, part_b, global_new, momentum_new)
    )
    sum_a = exchanged(part_a, YZ)
    sum_b = terms_along(blocks_along(part_b, X, 0), X)
    gradient = jnp.concatenate([total(sum_a), total(sum_b)], 1)

    first_new = beta_one * adam_first[0] + (1.0 - beta_one) * gradient
    second_new = beta_two * adam_second[0] + (1.0 - beta_two) * gradient * gradient
    adam_step = (
        first_new / correct_one / (jnp.sqrt(second_new / correct_two) + adam_eps)
        + weight_decay * own_local
    )
    merged = (global_new - inner_rate * adam_step).astype(jnp.bfloat16)
    merged_a, merged_b = merged[:cut], merged[cut:]
    near_b = placed_along(merged_b, X)
    near_a, near_b = lax.optimization_barrier((exchanged(copies(merged_a, plane), YZ), near_b))
    all_a = [n.reshape(ny, nz, cut, width) for n in arrived_along(near_a, X)]
    all_b = exchanged(copies(near_b, plane), YZ).reshape(ny, nz, nx, rows - cut, width)
    gathered = joined(all_a, all_b, lax.axis_index(X))
    return (gathered[None], global_new, momentum_new[None], first_new[None], second_new[None])


def solution(mesh):
    torus = Mesh(
        mesh.devices.reshape(mesh.shape["replica"] // 2, 2, 8, 4, 4), REPLICA + DP
    )
    in_specs = (
        P(REPLICA, DP, None),
        P(REPLICA, DP, None),
        P(REPLICA, DP, None),
        P(DP, None),
        P(DP, REPLICA, None),
        P(REPLICA, DP, None),
        P(REPLICA, DP, None),
    )
    out_specs = (
        P(REPLICA, None, None),
        P(DP, None),
        P(DP, REPLICA, None),
        P(REPLICA, DP, None),
        P(REPLICA, DP, None),
    )
    return jax.shard_map(
        per_device, mesh=torus, in_specs=in_specs, out_specs=out_specs, check_vma=False
    )
```

```python
import jax
import jax.numpy as jnp
from jax import lax
from jax.experimental import pallas as pl
from jax.experimental.pallas import tpu as pltpu
from jax.sharding import Mesh
from jax.sharding import PartitionSpec as P

DP = ("dp_0", "dp_1", "dp_2")
YZ = ("dp_0", "dp_2")
X = "dp_1"
HI, CORE = REPLICA = ("chip", "core")

outer_mu = 0.9
outer_rate = 0.7
beta_one = 0.9
beta_two = 0.95
adam_eps = 1e-08
weight_decay = 0.1
inner_rate = 0.1
correct_one = 1.0 - 0.9**50
correct_two = 1.0 - 0.95**50


def exchanged(x, axes):
    return lax.all_to_all(x, axes, 0, 0, tiled=True)


def copies(x, n):
    return jnp.broadcast_to(x[None], (n, *x.shape))


def total(blocks):
    parts = [b.astype(jnp.float32) for b in blocks]
    while len(parts) > 1:
        parts = [sum(parts[i : i + 2]) for i in range(0, len(parts), 2)]
    return parts[0]


def passed(x, axis, step):
    n = lax.axis_size(axis)
    return lax.ppermute(x, axis, [(i, (i + step) % n) for i in range(n)])


def turned(index, n):
    return index & (n - 1) if n & (n - 1) == 0 else lax.rem(index, n)


def block_of(x, index, dim):
    return lax.dynamic_index_in_dim(x, index, dim, keepdims=False)


def arrived_along(x, axis):
    return [x] + [passed(x, axis, k) for k in range(1, lax.axis_size(axis))]


def in_order(arrived, axis):
    n = lax.axis_size(axis)
    me = lax.axis_index(axis)
    blocks = jnp.stack(arrived)
    return jnp.stack([block_of(blocks, turned(me + n - i, n), 0) for i in range(n)])


def placed_along(x, axis):
    return in_order(arrived_along(x, axis), axis)


def joining(me_ref, *refs):
    *near, far, out, near_in, far_in, held, got, sent = refs
    places = len(near)
    ny = far.shape[0]
    me = me_ref[0]

    def loads(y):
        return [
            pltpu.make_async_copy(ref.at[y], near_in.at[k, y], got.at[k, y])
            for k, ref in enumerate(near)
        ] + [pltpu.make_async_copy(far.at[y], far_in.at[y], got.at[places, y])]

    def store(y):
        return pltpu.make_async_copy(held.at[y], out.at[y], sent.at[y])

    for y in range(ny):
        for copy in loads(y):
            copy.start()
    for y in range(ny):
        for copy in loads(y):
            copy.wait()
        for k in range(places):
            x = turned(me + places - k, places)
            both = jnp.concatenate(
                [near_in[k, y].astype(jnp.float32), far_in[y, :, x].astype(jnp.float32)], axis=1
            )
            held[y, x] = both.reshape(-1, both.shape[-1]).astype(out.dtype)
        store(y).start()
    for y in range(ny):
        store(y).wait()


def joined(near, far, me):
    ny, nz, cut, width = near[0].shape
    nx, rest = far.shape[2:4]
    shape = (ny, nx, nz * (cut + rest), width)
    place = pl.BlockSpec(memory_space=pl.ANY)
    out = pl.pallas_call(
        joining,
        in_specs=[pl.BlockSpec(memory_space=pltpu.SMEM)] + [place] * (nx + 1),
        out_specs=place,
        out_shape=jax.ShapeDtypeStruct(shape, far.dtype),
        scratch_shapes=[
            pltpu.VMEM((nx, *near[0].shape), far.dtype),
            pltpu.VMEM(far.shape, far.dtype),
            pltpu.VMEM(shape, far.dtype),
            pltpu.SemaphoreType.DMA((nx + 1, ny)),
            pltpu.SemaphoreType.DMA((ny,)),
        ],
        name="joined",
    )(me.reshape(1), *near, far)
    return out.reshape(-1, width)


def per_device(
    layer_input, key_cotangent, local_params, global_params, outer_momentum, adam_first, adam_second
):
    features = layer_input[0]
    cotangent = key_cotangent[0]
    own_local = local_params[0]
    rows, width = global_params.shape
    ny, nx, nz = (lax.axis_size(a) for a in DP)
    plane = ny * nz
    n_hi, n_core = lax.axis_size(HI), lax.axis_size(CORE)
    replicas = n_hi * n_core
    sub_rows = outer_momentum.shape[1]
    cut = rows * 2 // 3

    core = lax.axis_index(CORE)
    hi = lax.axis_index(HI)
    deltas = global_params - own_local
    mine = jnp.concatenate([deltas, outer_momentum[0]], 0)
    other = passed(mine, CORE, 1)

    term = lax.dot_general(
        features, cotangent, (((0,), (0,)), ((), ())), preferred_element_type=jnp.float32
    ).astype(jnp.float16)
    along_x = exchanged(term.reshape(ny, nx, nz * rows, width).transpose(1, 0, 2, 3), X)

    upper, lower = jnp.where(core == 0, mine, other), jnp.where(core == 0, other, mine)
    pair = jnp.concatenate([mine[:rows] + other[:rows], upper[rows:], lower[rows:]], 0)
    along_x, chips = lax.optimization_barrier((along_x, arrived_along(pair, HI)))
    by_chip = in_order(chips, HI)
    outer_grad = sum(p[:rows] for p in by_chip) / replicas
    old_rows = jnp.concatenate([p[rows:] for p in by_chip], 0)
    momentum_all = outer_mu * old_rows + outer_grad
    global_new = global_params - outer_rate * (outer_grad + outer_mu * momentum_all)
    momentum_new = lax.dynamic_slice_in_dim(
        momentum_all, (hi * n_core + core) * sub_rows, sub_rows, 0
    )

    part = total(along_x).astype(jnp.float16).reshape(plane, rows, width)
    gradient = total(exchanged(part, YZ))

    first_new = beta_one * adam_first[0] + (1.0 - beta_one) * gradient
    second_new = beta_two * adam_second[0] + (1.0 - beta_two) * gradient * gradient
    adam_step = (
        first_new / correct_one / (jnp.sqrt(second_new / correct_two) + adam_eps)
        + weight_decay * own_local
    )
    merged = (global_new - inner_rate * adam_step).astype(jnp.bfloat16)
    merged_a, merged_b = merged[:cut], merged[cut:]
    near_b = placed_along(merged_b, X)
    near_a, near_b = lax.optimization_barrier((exchanged(copies(merged_a, plane), YZ), near_b))
    all_a = [n.reshape(ny, nz, cut, width) for n in arrived_along(near_a, X)]
    all_b = exchanged(copies(near_b, plane), YZ).reshape(ny, nz, nx, rows - cut, width)
    gathered = joined(all_a, all_b, lax.axis_index(X))
    return (gathered[None], global_new, momentum_new[None], first_new[None], second_new[None])


def solution(mesh):
    torus = Mesh(
        mesh.devices.reshape(mesh.shape["replica"] // 2, 2, 8, 4, 4), REPLICA + DP
    )
    in_specs = (
        P(REPLICA, DP, None),
        P(REPLICA, DP, None),
        P(REPLICA, DP, None),
        P(DP, None),
        P(DP, REPLICA, None),
        P(REPLICA, DP, None),
        P(REPLICA, DP, None),
    )
    out_specs = (
        P(REPLICA, None, None),
        P(DP, None),
        P(DP, REPLICA, None),
        P(REPLICA, DP, None),
        P(REPLICA, DP, None),
    )
    return jax.shard_map(
        per_device, mesh=torus, in_specs=in_specs, out_specs=out_specs, check_vma=False
    )
```

```python
import jax
import jax.numpy as jnp
from jax import lax
from jax.experimental import pallas as pl
from jax.experimental.pallas import tpu as pltpu
from jax.sharding import Mesh
from jax.sharding import PartitionSpec as P

DP = ("dp_0", "dp_1", "dp_2")
YZ = ("dp_0", "dp_2")
X = "dp_1"
HI, CORE = REPLICA = ("chip", "core")

outer_mu = 0.9
outer_rate = 0.7
beta_one = 0.9
beta_two = 0.95
adam_eps = 1e-08
weight_decay = 0.1
inner_rate = 0.1
correct_one = 1.0 - 0.9**50
correct_two = 1.0 - 0.95**50


def exchanged(x, axes):
    return lax.all_to_all(x, axes, 0, 0, tiled=True)


def copies(x, n):
    return jnp.broadcast_to(x[None], (n, *x.shape))


def total(blocks):
    parts = [b.astype(jnp.float32) for b in blocks]
    while len(parts) > 1:
        parts = [sum(parts[i : i + 2]) for i in range(0, len(parts), 2)]
    return parts[0]


def passed(x, axis, step):
    n = lax.axis_size(axis)
    return lax.ppermute(x, axis, [(i, (i + step) % n) for i in range(n)])


def turned(index, n):
    return index & (n - 1) if n & (n - 1) == 0 else lax.rem(index, n)


def block_of(x, index, dim):
    return lax.dynamic_index_in_dim(x, index, dim, keepdims=False)


def arrived_along(x, axis):
    return [x] + [passed(x, axis, k) for k in range(1, lax.axis_size(axis))]


def in_order(arrived, axis):
    n = lax.axis_size(axis)
    me = lax.axis_index(axis)
    blocks = jnp.stack(arrived)
    return jnp.stack([block_of(blocks, turned(me + n - i, n), 0) for i in range(n)])


def placed_along(x, axis):
    return in_order(arrived_along(x, axis), axis)


def joining(near, far, out, near_in, far_in, held, got, sent):
    places, ny = near.shape[:2]

    def loads(y):
        return [
            pltpu.make_async_copy(near.at[x, y], near_in.at[x, y], got.at[x, y])
            for x in range(places)
        ] + [pltpu.make_async_copy(far.at[y], far_in.at[y], got.at[places, y])]

    def store(y):
        return pltpu.make_async_copy(held.at[y], out.at[y], sent.at[y])

    for y in range(ny):
        for copy in loads(y):
            copy.start()
    for y in range(ny):
        for copy in loads(y):
            copy.wait()
        for x in range(places):
            both = jnp.concatenate(
                [near_in[x, y].astype(jnp.float32), far_in[y, :, x].astype(jnp.float32)], axis=1
            )
            held[y, x] = both.reshape(-1, both.shape[-1]).astype(out.dtype)
        store(y).start()
    for y in range(ny):
        store(y).wait()


def joined(near, far):
    nx, ny, nz, cut, width = near.shape
    shape = (ny, nx, nz * (cut + far.shape[3]), width)
    place = pl.BlockSpec(memory_space=pl.ANY)
    out = pl.pallas_call(
        joining,
        in_specs=[place, place],
        out_specs=place,
        out_shape=jax.ShapeDtypeStruct(shape, far.dtype),
        scratch_shapes=[
            pltpu.VMEM(near.shape, far.dtype),
            pltpu.VMEM(far.shape, far.dtype),
            pltpu.VMEM(shape, far.dtype),
            pltpu.SemaphoreType.DMA((nx + 1, ny)),
            pltpu.SemaphoreType.DMA((ny,)),
        ],
        name="joined",
    )(near, far)
    return out.reshape(-1, width)


def per_device(
    layer_input, key_cotangent, local_params, global_params, outer_momentum, adam_first, adam_second
):
    features = layer_input[0]
    cotangent = key_cotangent[0]
    own_local = local_params[0]
    rows, width = global_params.shape
    ny, nx, nz = (lax.axis_size(a) for a in DP)
    plane = ny * nz
    n_hi, n_core = lax.axis_size(HI), lax.axis_size(CORE)
    replicas = n_hi * n_core
    sub_rows = outer_momentum.shape[1]
    cut = rows * 2 // 3

    core = lax.axis_index(CORE)
    hi = lax.axis_index(HI)
    deltas = global_params - own_local
    mine = jnp.concatenate([deltas, outer_momentum[0]], 0)
    other = passed(mine, CORE, 1)

    term = lax.dot_general(
        features, cotangent, (((0,), (0,)), ((), ())), preferred_element_type=jnp.float32
    ).astype(jnp.float16)
    along_x = exchanged(term.reshape(ny, nx, nz * rows, width).transpose(1, 0, 2, 3), X)

    upper, lower = jnp.where(core == 0, mine, other), jnp.where(core == 0, other, mine)
    pair = jnp.concatenate([mine[:rows] + other[:rows], upper[rows:], lower[rows:]], 0)
    along_x, chips = lax.optimization_barrier((along_x, arrived_along(pair, HI)))
    by_chip = in_order(chips, HI)
    outer_grad = sum(p[:rows] for p in by_chip) / replicas
    old_rows = jnp.concatenate([p[rows:] for p in by_chip], 0)
    momentum_all = outer_mu * old_rows + outer_grad
    global_new = global_params - outer_rate * (outer_grad + outer_mu * momentum_all)
    momentum_new = lax.dynamic_slice_in_dim(
        momentum_all, (hi * n_core + core) * sub_rows, sub_rows, 0
    )

    part = total(along_x).astype(jnp.float16).reshape(plane, rows, width)
    gradient = total(exchanged(part, YZ))

    first_new = beta_one * adam_first[0] + (1.0 - beta_one) * gradient
    second_new = beta_two * adam_second[0] + (1.0 - beta_two) * gradient * gradient
    adam_step = (
        first_new / correct_one / (jnp.sqrt(second_new / correct_two) + adam_eps)
        + weight_decay * own_local
    )
    merged = (global_new - inner_rate * adam_step).astype(jnp.bfloat16)
    merged_a, merged_b = merged[:cut], merged[cut:]
    near_b = placed_along(merged_b, X)
    near_a, near_b = lax.optimization_barrier((exchanged(copies(merged_a, plane), YZ), near_b))
    all_a = lax.all_gather(near_a, X).reshape(nx, ny, nz, cut, width)
    all_b = exchanged(copies(near_b, plane), YZ).reshape(ny, nz, nx, rows - cut, width)
    gathered = joined(all_a, all_b)
    return (gathered[None], global_new, momentum_new[None], first_new[None], second_new[None])


def solution(mesh):
    torus = Mesh(
        mesh.devices.reshape(mesh.shape["replica"] // 2, 2, 8, 4, 4), REPLICA + DP
    )
    in_specs = (
        P(REPLICA, DP, None),
        P(REPLICA, DP, None),
        P(REPLICA, DP, None),
        P(DP, None),
        P(DP, REPLICA, None),
        P(REPLICA, DP, None),
        P(REPLICA, DP, None),
    )
    out_specs = (
        P(REPLICA, None, None),
        P(DP, None),
        P(DP, REPLICA, None),
        P(REPLICA, DP, None),
        P(REPLICA, DP, None),
    )
    return jax.shard_map(
        per_device, mesh=torus, in_specs=in_specs, out_specs=out_specs, check_vma=False
    )
```

```python
import jax
import jax.numpy as jnp
import numpy as np
from jax import lax
from jax.sharding import Mesh
from jax.sharding import PartitionSpec as P

DP = ("dp_0", "dp_1", "dp_2")
HI, CORE = REPLICA = ("chip", "core")

outer_mu = 0.9
outer_rate = 0.7
beta_one = 0.9
beta_two = 0.95
adam_eps = 1e-08
weight_decay = 0.1
inner_rate = 0.1
correct_one = 1.0 - 0.9**50
correct_two = 1.0 - 0.95**50


def exchanged(x, groups):
    return lax.all_to_all(x, REPLICA + DP, 0, 0, axis_index_groups=groups, tiled=True)


def copies(x, n):
    return jnp.broadcast_to(x[None], (n, *x.shape))


def total(blocks):
    parts = [b.astype(jnp.float32) for b in blocks]
    while len(parts) > 1:
        parts = [sum(parts[i : i + 2]) for i in range(0, len(parts), 2)]
    return parts[0]


def passed(x, axis, step):
    n = lax.axis_size(axis)
    return lax.ppermute(x, axis, [(i, (i + step) % n) for i in range(n)])


def turned(index, n):
    return index & (n - 1) if n & (n - 1) == 0 else lax.rem(index, n)


def block_of(x, index, dim):
    return lax.dynamic_index_in_dim(x, index, dim, keepdims=False)


def arrived_along(x, axis):
    return [x] + [passed(x, axis, k) for k in range(1, lax.axis_size(axis))]


def in_order(arrived, axis):
    n = lax.axis_size(axis)
    me = lax.axis_index(axis)
    blocks = jnp.stack(arrived)
    return jnp.stack([block_of(blocks, turned(me + n - i, n), 0) for i in range(n)])


def crossing_groups(replicas, sizes, n_core):
    ny, nx, nz = sizes
    dp = ny * nx * nz
    at = np.arange(dp).reshape(ny, nx, nz)
    tables = (
        at.transpose(1, 0, 2).reshape(nx, -1),
        at.reshape(ny // 2, 2, nx, nz // 2, 2).transpose(1, 4, 0, 2, 3).reshape(4, -1),
    )
    near, far = [], []
    for replica in range(replicas):
        table = tables[replica % n_core] + replica * dp
        near += table.T.tolist()
        far += table.tolist()
    return near, far


def per_core(core, ways, x):
    return lax.cond(core == 0, ways[0], ways[1], x)


def per_device(
    layer_input, key_cotangent, local_params, global_params, outer_momentum, adam_first, adam_second
):
    features = layer_input[0]
    cotangent = key_cotangent[0]
    own_local = local_params[0]
    rows, width = global_params.shape
    ny, nx, nz = (lax.axis_size(a) for a in DP)
    plane = ny * nz
    n_hi, n_core = lax.axis_size(HI), lax.axis_size(CORE)
    replicas = n_hi * n_core
    sub_rows = outer_momentum.shape[1]
    near, far = crossing_groups(replicas, (ny, nx, nz), n_core)

    core = lax.axis_index(CORE)
    hi = lax.axis_index(HI)
    deltas = global_params - own_local
    mine = jnp.concatenate([deltas, outer_momentum[0]], 0)
    other = passed(mine, CORE, 1)

    term = lax.dot_general(
        features, cotangent, (((0,), (0,)), ((), ())), preferred_element_type=jnp.float32
    ).astype(jnp.float16)
    blocks = per_core(
        core,
        (
            lambda t: t.reshape(ny, nx, nz * rows, width).transpose(1, 0, 2, 3).reshape(4, -1, rows, width),
            lambda t: t.reshape(ny // 2, 2, nx, nz // 2, 2, rows, width)
            .transpose(1, 4, 0, 2, 3, 5, 6)
            .reshape(4, -1, rows, width),
        ),
        term,
    )
    summed_near = exchanged(blocks, near)

    upper, lower = jnp.where(core == 0, mine, other), jnp.where(core == 0, other, mine)
    pair = jnp.concatenate([mine[:rows] + other[:rows], upper[rows:], lower[rows:]], 0)
    summed_near, chips = lax.optimization_barrier((summed_near, arrived_along(pair, HI)))
    by_chip = in_order(chips, HI)
    outer_grad = sum(p[:rows] for p in by_chip) / replicas
    old_rows = jnp.concatenate([p[rows:] for p in by_chip], 0)
    momentum_all = outer_mu * old_rows + outer_grad
    global_new = global_params - outer_rate * (outer_grad + outer_mu * momentum_all)
    momentum_new = lax.dynamic_slice_in_dim(
        momentum_all, (hi * n_core + core) * sub_rows, sub_rows, 0
    )

    part = total(summed_near).astype(jnp.float16)
    gradient = total(exchanged(part, far))

    first_new = beta_one * adam_first[0] + (1.0 - beta_one) * gradient
    second_new = beta_two * adam_second[0] + (1.0 - beta_two) * gradient * gradient
    adam_step = (
        first_new / correct_one / (jnp.sqrt(second_new / correct_two) + adam_eps)
        + weight_decay * own_local
    )
    merged = (global_new - inner_rate * adam_step).astype(jnp.bfloat16)
    held = exchanged(copies(merged, plane), far)
    held = exchanged(copies(held, nx), near)
    gathered = per_core(
        core,
        (
            lambda t: t.reshape(nx, ny, nz * rows, width).transpose(1, 0, 2, 3).reshape(-1, width),
            lambda t: t.reshape(2, 2, ny // 2, nx, nz // 2, rows, width)
            .transpose(2, 0, 3, 4, 1, 5, 6)
            .reshape(-1, width),
        ),
        held,
    )
    return (gathered[None], global_new, momentum_new[None], first_new[None], second_new[None])


def solution(mesh):
    torus = Mesh(
        mesh.devices.reshape(mesh.shape["replica"] // 2, 2, 8, 4, 4), REPLICA + DP
    )
    in_specs = (
        P(REPLICA, DP, None),
        P(REPLICA, DP, None),
        P(REPLICA, DP, None),
        P(DP, None),
        P(DP, REPLICA, None),
        P(REPLICA, DP, None),
        P(REPLICA, DP, None),
    )
    out_specs = (
        P(REPLICA, None, None),
        P(DP, None),
        P(DP, REPLICA, None),
        P(REPLICA, DP, None),
        P(REPLICA, DP, None),
    )
    return jax.shard_map(
        per_device, mesh=torus, in_specs=in_specs, out_specs=out_specs, check_vma=False
    )
```

```python
import math
from functools import partial

import jax
import jax.numpy as jnp
import numpy as np
from jax import lax
from jax.sharding import Mesh
from jax.sharding import PartitionSpec as P

DP = ("dp_0", "dp_1", "dp_2")
HI, CORE = REPLICA = ("chip", "core")

outer_mu = 0.9
outer_rate = 0.7
beta_one = 0.9
beta_two = 0.95
adam_eps = 1e-08
weight_decay = 0.1
inner_rate = 0.1
correct_one = 1.0 - 0.9**50
correct_two = 1.0 - 0.95**50


def exchanged(x, groups):
    return lax.all_to_all(x, REPLICA + DP, 0, 0, axis_index_groups=groups, tiled=True)


def copies(x, n):
    return jnp.broadcast_to(x[None], (n, *x.shape))


def total(blocks):
    parts = [b.astype(jnp.float32) for b in blocks]
    while len(parts) > 1:
        parts = [sum(parts[i : i + 2]) for i in range(0, len(parts), 2)]
    return parts[0]


def passed(x, axis, step):
    n = lax.axis_size(axis)
    return lax.ppermute(x, axis, [(i, (i + step) % n) for i in range(n)])


def turned(index, n):
    return index & (n - 1) if n & (n - 1) == 0 else lax.rem(index, n)


def block_of(x, index, dim):
    return lax.dynamic_index_in_dim(x, index, dim, keepdims=False)


def arrived_along(x, axis):
    return [x] + [passed(x, axis, k) for k in range(1, lax.axis_size(axis))]


def in_order(arrived, axis):
    n = lax.axis_size(axis)
    me = lax.axis_index(axis)
    blocks = jnp.stack(arrived)
    return jnp.stack([block_of(blocks, turned(me + n - i, n), 0) for i in range(n)])


ORDERS = ((2, 1, 4, 0, 3), (1, 4, 2, 0, 3))


def crossing_groups(replicas, sizes, n_core):
    split = (sizes[0] // 2, 2, sizes[1], sizes[2] // 2, 2)
    dp = math.prod(split)
    stages = [], [], []
    for replica in range(replicas):
        at = np.arange(dp).reshape(split).transpose(ORDERS[replica % n_core])
        at = at.reshape(4, 4, -1) + replica * dp
        for stage in range(3):
            stages[stage].extend(np.moveaxis(at, stage, -1).reshape(-1, at.shape[stage]).tolist())
    return stages


def to_places(order, split, x):
    parts = x.reshape(*split, -1, x.shape[-1])
    return parts.transpose(*order, 5, 6).reshape(4, 4, -1, *parts.shape[5:])


def from_places(order, split, x):
    parts = x.reshape(*(split[k] for k in order), *x.shape[-2:])
    return parts.transpose(*(order.index(k) for k in range(5)), 5, 6).reshape(-1, x.shape[-1])


def per_core(core, way, split, x):
    return lax.cond(core == 0, partial(way, ORDERS[0], split), partial(way, ORDERS[1], split), x)


def per_device(
    layer_input, key_cotangent, local_params, global_params, outer_momentum, adam_first, adam_second
):
    features = layer_input[0]
    cotangent = key_cotangent[0]
    own_local = local_params[0]
    rows, width = global_params.shape
    ny, nx, nz = (lax.axis_size(a) for a in DP)
    n_hi, n_core = lax.axis_size(HI), lax.axis_size(CORE)
    replicas = n_hi * n_core
    sub_rows = outer_momentum.shape[1]
    near, middle, far = crossing_groups(replicas, (ny, nx, nz), n_core)
    split = (ny // 2, 2, nx, nz // 2, 2)

    core = lax.axis_index(CORE)
    hi = lax.axis_index(HI)
    deltas = global_params - own_local
    mine = jnp.concatenate([deltas, outer_momentum[0]], 0)
    other = passed(mine, CORE, 1)

    term = lax.dot_general(
        features, cotangent, (((0,), (0,)), ((), ())), preferred_element_type=jnp.float32
    ).astype(jnp.float16)
    blocks = per_core(core, to_places, split, term)
    summed_near = exchanged(blocks, near)

    upper, lower = jnp.where(core == 0, mine, other), jnp.where(core == 0, other, mine)
    pair = jnp.concatenate([mine[:rows] + other[:rows], upper[rows:], lower[rows:]], 0)
    summed_near, chips = lax.optimization_barrier((summed_near, arrived_along(pair, HI)))
    by_chip = in_order(chips, HI)
    outer_grad = sum(p[:rows] for p in by_chip) / replicas
    old_rows = jnp.concatenate([p[rows:] for p in by_chip], 0)
    momentum_all = outer_mu * old_rows + outer_grad
    global_new = global_params - outer_rate * (outer_grad + outer_mu * momentum_all)
    momentum_new = lax.dynamic_slice_in_dim(
        momentum_all, (hi * n_core + core) * sub_rows, sub_rows, 0
    )

    part = total(summed_near).astype(jnp.float16)
    part = total(exchanged(part, middle)).astype(jnp.float16)
    gradient = total(exchanged(part, far))

    first_new = beta_one * adam_first[0] + (1.0 - beta_one) * gradient
    second_new = beta_two * adam_second[0] + (1.0 - beta_two) * gradient * gradient
    adam_step = (
        first_new / correct_one / (jnp.sqrt(second_new / correct_two) + adam_eps)
        + weight_decay * own_local
    )
    merged = (global_new - inner_rate * adam_step).astype(jnp.bfloat16)
    held = merged
    for groups in (far, middle, near):
        held = exchanged(copies(held, len(groups[0])), groups)
    gathered = per_core(core, from_places, split, held)
    return (gathered[None], global_new, momentum_new[None], first_new[None], second_new[None])


def solution(mesh):
    torus = Mesh(
        mesh.devices.reshape(mesh.shape["replica"] // 2, 2, 8, 4, 4), REPLICA + DP
    )
    in_specs = (
        P(REPLICA, DP, None),
        P(REPLICA, DP, None),
        P(REPLICA, DP, None),
        P(DP, None),
        P(DP, REPLICA, None),
        P(REPLICA, DP, None),
        P(REPLICA, DP, None),
    )
    out_specs = (
        P(REPLICA, None, None),
        P(DP, None),
        P(DP, REPLICA, None),
        P(REPLICA, DP, None),
        P(REPLICA, DP, None),
    )
    return jax.shard_map(
        per_device, mesh=torus, in_specs=in_specs, out_specs=out_specs, check_vma=False
    )
```

```python
import math
from functools import partial

import jax
import jax.numpy as jnp
import numpy as np
from jax import lax
from jax.sharding import Mesh
from jax.sharding import PartitionSpec as P

DP = ("dp_0", "dp_1", "dp_2")
HI, CORE = REPLICA = ("chip", "core")

outer_mu = 0.9
outer_rate = 0.7
beta_one = 0.9
beta_two = 0.95
adam_eps = 1e-08
weight_decay = 0.1
inner_rate = 0.1
correct_one = 1.0 - 0.9**50
correct_two = 1.0 - 0.95**50


def exchanged(x, groups):
    return lax.all_to_all(x, REPLICA + DP, 0, 0, axis_index_groups=groups, tiled=True)


def copies(x, n):
    return jnp.broadcast_to(x[None], (n, *x.shape))


def total(blocks):
    parts = [b.astype(jnp.float32) for b in blocks]
    while len(parts) > 1:
        parts = [sum(parts[i : i + 2]) for i in range(0, len(parts), 2)]
    return parts[0]


def passed(x, axis, step):
    n = lax.axis_size(axis)
    return lax.ppermute(x, axis, [(i, (i + step) % n) for i in range(n)])


def turned(index, n):
    return index & (n - 1) if n & (n - 1) == 0 else lax.rem(index, n)


def block_of(x, index, dim):
    return lax.dynamic_index_in_dim(x, index, dim, keepdims=False)


def arrived_along(x, axis):
    return [x] + [passed(x, axis, k) for k in range(1, lax.axis_size(axis))]


def in_order(arrived, axis):
    n = lax.axis_size(axis)
    me = lax.axis_index(axis)
    blocks = jnp.stack(arrived)
    return jnp.stack([block_of(blocks, turned(me + n - i, n), 0) for i in range(n)])


ORDERS = ((2, 1, 4, 0, 3), (1, 4, 2, 0, 3))


def crossing_groups(replicas, sizes, n_core):
    split = (sizes[0] // 2, 2, sizes[1], sizes[2] // 2, 2)
    dp = math.prod(split)
    stages = [], [], []
    for replica in range(replicas):
        at = np.arange(dp).reshape(split).transpose(ORDERS[replica % n_core])
        at = at.reshape(4, 4, -1) + replica * dp
        for stage in range(3):
            stages[stage].extend(np.moveaxis(at, stage, -1).reshape(-1, at.shape[stage]).tolist())
    return stages


def to_places(order, split, x):
    parts = x.reshape(*split, -1, x.shape[-1])
    return parts.transpose(*order, 5, 6).reshape(4, 4, -1, *parts.shape[5:])


def from_places(order, split, x):
    parts = x.reshape(*(split[k] for k in order), *x.shape[-2:])
    return parts.transpose(*(order.index(k) for k in range(5)), 5, 6).reshape(-1, x.shape[-1])


def per_core(core, way, split, x):
    return lax.cond(core == 0, partial(way, ORDERS[0], split), partial(way, ORDERS[1], split), x)


def per_device(
    layer_input, key_cotangent, local_params, global_params, outer_momentum, adam_first, adam_second
):
    features = layer_input[0]
    cotangent = key_cotangent[0]
    own_local = local_params[0]
    rows, width = global_params.shape
    ny, nx, nz = (lax.axis_size(a) for a in DP)
    n_hi, n_core = lax.axis_size(HI), lax.axis_size(CORE)
    replicas = n_hi * n_core
    sub_rows = outer_momentum.shape[1]
    near, middle, far = crossing_groups(replicas, (ny, nx, nz), n_core)
    split = (ny // 2, 2, nx, nz // 2, 2)

    core = lax.axis_index(CORE)
    hi = lax.axis_index(HI)
    chips = arrived_along(jnp.concatenate([own_local, outer_momentum[0]], 0), HI)

    term = lax.dot_general(
        features, cotangent, (((0,), (0,)), ((), ())), preferred_element_type=jnp.float32
    ).astype(jnp.float16)
    blocks = per_core(core, to_places, split, term)
    summed_near = exchanged(blocks, near)

    summed_near, chips = lax.optimization_barrier((summed_near, chips))
    by_chip = in_order(chips, HI)
    summed = jnp.concatenate(
        [sum(global_params - c[:rows] for c in by_chip)] + [c[rows:] for c in by_chip], 0
    )
    other = passed(summed, CORE, 1)
    outer_grad = (summed[:rows] + other[:rows]) / replicas
    upper, lower = jnp.where(core == 0, summed, other), jnp.where(core == 0, other, summed)
    old_rows = jnp.concatenate(
        [
            side[lo : lo + sub_rows]
            for lo in range(rows, rows + n_hi * sub_rows, sub_rows)
            for side in (upper, lower)
        ],
        0,
    )
    momentum_all = outer_mu * old_rows + outer_grad
    global_new = global_params - outer_rate * (outer_grad + outer_mu * momentum_all)
    momentum_new = lax.dynamic_slice_in_dim(
        momentum_all, (hi * n_core + core) * sub_rows, sub_rows, 0
    )

    part = total(summed_near).astype(jnp.float16)
    part = total(exchanged(part, middle)).astype(jnp.float16)
    gradient = total(exchanged(part, far))

    first_new = beta_one * adam_first[0] + (1.0 - beta_one) * gradient
    second_new = beta_two * adam_second[0] + (1.0 - beta_two) * gradient * gradient
    adam_step = (
        first_new / correct_one / (jnp.sqrt(second_new / correct_two) + adam_eps)
        + weight_decay * own_local
    )
    merged = (global_new - inner_rate * adam_step).astype(jnp.bfloat16)
    held = merged
    for groups in (far, middle, near):
        held = exchanged(copies(held, len(groups[0])), groups)
    gathered = per_core(core, from_places, split, held)
    return (gathered[None], global_new, momentum_new[None], first_new[None], second_new[None])


def solution(mesh):
    torus = Mesh(
        mesh.devices.reshape(mesh.shape["replica"] // 2, 2, 8, 4, 4), REPLICA + DP
    )
    in_specs = (
        P(REPLICA, DP, None),
        P(REPLICA, DP, None),
        P(REPLICA, DP, None),
        P(DP, None),
        P(DP, REPLICA, None),
        P(REPLICA, DP, None),
        P(REPLICA, DP, None),
    )
    out_specs = (
        P(REPLICA, None, None),
        P(DP, None),
        P(DP, REPLICA, None),
        P(REPLICA, DP, None),
        P(REPLICA, DP, None),
    )
    return jax.shard_map(
        per_device, mesh=torus, in_specs=in_specs, out_specs=out_specs, check_vma=False
    )
```

```python
import math
from functools import partial

import jax
import jax.numpy as jnp
import numpy as np
from jax import lax
from jax.experimental import pallas as pl
from jax.experimental.pallas import tpu as pltpu
from jax.sharding import Mesh
from jax.sharding import PartitionSpec as P

DP = ("dp_0", "dp_1", "dp_2")
HI, CORE = REPLICA = ("chip", "core")

outer_mu = 0.9
outer_rate = 0.7
beta_one = 0.9
beta_two = 0.95
adam_eps = 1e-08
weight_decay = 0.1
inner_rate = 0.1
correct_one = 1.0 - 0.9**50
correct_two = 1.0 - 0.95**50


def exchanged(x, groups):
    return lax.all_to_all(x, REPLICA + DP, 0, 0, axis_index_groups=groups, tiled=True)


def copies(x, n):
    return jnp.broadcast_to(x[None], (n, *x.shape))


def total(blocks):
    parts = [b.astype(jnp.float32) for b in blocks]
    while len(parts) > 1:
        parts = [sum(parts[i : i + 2]) for i in range(0, len(parts), 2)]
    return parts[0]


def passed(x, axis, step):
    n = lax.axis_size(axis)
    return lax.ppermute(x, axis, [(i, (i + step) % n) for i in range(n)])


def turned(index, n):
    return index & (n - 1) if n & (n - 1) == 0 else lax.rem(index, n)


def block_of(x, index, dim):
    return lax.dynamic_index_in_dim(x, index, dim, keepdims=False)


def arrived_along(x, axis):
    return [x] + [passed(x, axis, k) for k in range(1, lax.axis_size(axis))]


def in_order(arrived, axis):
    n = lax.axis_size(axis)
    me = lax.axis_index(axis)
    blocks = jnp.stack(arrived)
    return jnp.stack([block_of(blocks, turned(me + n - i, n), 0) for i in range(n)])


ORDERS = ((2, 1, 4, 0, 3), (1, 4, 2, 0, 3))


def crossing_groups(replicas, sizes, n_core):
    split = (sizes[0] // 2, 2, sizes[1], sizes[2] // 2, 2)
    dp = math.prod(split)
    stages = [], [], []
    for replica in range(replicas):
        at = np.arange(dp).reshape(split).transpose(ORDERS[replica % n_core])
        at = at.reshape(4, 4, -1) + replica * dp
        for stage in range(3):
            stages[stage].extend(np.moveaxis(at, stage, -1).reshape(-1, at.shape[stage]).tolist())
    return stages


def to_places(order, split, x):
    parts = x.reshape(*split, -1, x.shape[-1])
    return parts.transpose(*order, 5, 6).reshape(4, 4, -1, *parts.shape[5:])


def placing(places, blocks, out, sent):
    count = blocks.shape[0]
    moves = [
        pltpu.make_async_copy(blocks.at[i], out.at[places[i]], sent.at[i]) for i in range(count)
    ]
    for move in moves:
        move.start()
    for move in moves:
        move.wait()


def placed(blocks, places):
    anywhere = pl.BlockSpec(memory_space=pl.ANY)
    return pl.pallas_call(
        placing,
        in_specs=[pl.BlockSpec(memory_space=pltpu.SMEM), anywhere],
        out_specs=anywhere,
        out_shape=jax.ShapeDtypeStruct(blocks.shape, blocks.dtype),
        scratch_shapes=[pltpu.SemaphoreType.DMA((blocks.shape[0],))],
        name="placed",
    )(places, blocks)


def per_core(core, way, split, x):
    return lax.cond(core == 0, partial(way, ORDERS[0], split), partial(way, ORDERS[1], split), x)


def per_device(
    layer_input, key_cotangent, local_params, global_params, outer_momentum, adam_first, adam_second
):
    features = layer_input[0]
    cotangent = key_cotangent[0]
    own_local = local_params[0]
    rows, width = global_params.shape
    ny, nx, nz = (lax.axis_size(a) for a in DP)
    n_hi, n_core = lax.axis_size(HI), lax.axis_size(CORE)
    replicas = n_hi * n_core
    sub_rows = outer_momentum.shape[1]
    near, middle, far = crossing_groups(replicas, (ny, nx, nz), n_core)
    split = (ny // 2, 2, nx, nz // 2, 2)

    core = lax.axis_index(CORE)
    hi = lax.axis_index(HI)
    chips = arrived_along(jnp.concatenate([own_local, outer_momentum[0]], 0), HI)

    term = lax.dot_general(
        features, cotangent, (((0,), (0,)), ((), ())), preferred_element_type=jnp.float32
    ).astype(jnp.float16)
    blocks = per_core(core, to_places, split, term)
    summed_near = exchanged(blocks, near)

    summed_near, chips = lax.optimization_barrier((summed_near, chips))
    by_chip = in_order(chips, HI)
    summed = jnp.concatenate(
        [sum(global_params - c[:rows] for c in by_chip)] + [c[rows:] for c in by_chip], 0
    )

    part = total(summed_near).astype(jnp.float16)
    part = exchanged(part, middle)
    part, summed = lax.optimization_barrier((part, summed))
    part = total(part).astype(jnp.float16)
    other = passed(summed, CORE, 1)
    outer_grad = (summed[:rows] + other[:rows]) / replicas
    upper, lower = jnp.where(core == 0, summed, other), jnp.where(core == 0, other, summed)
    old_rows = jnp.concatenate(
        [
            side[lo : lo + sub_rows]
            for lo in range(rows, rows + n_hi * sub_rows, sub_rows)
            for side in (upper, lower)
        ],
        0,
    )
    momentum_all = outer_mu * old_rows + outer_grad
    global_new = global_params - outer_rate * (outer_grad + outer_mu * momentum_all)
    momentum_new = lax.dynamic_slice_in_dim(
        momentum_all, (hi * n_core + core) * sub_rows, sub_rows, 0
    )

    gradient = total(exchanged(part, far))

    first_new = beta_one * adam_first[0] + (1.0 - beta_one) * gradient
    second_new = beta_two * adam_second[0] + (1.0 - beta_two) * gradient * gradient
    adam_step = (
        first_new / correct_one / (jnp.sqrt(second_new / correct_two) + adam_eps)
        + weight_decay * own_local
    )
    merged = (global_new - inner_rate * adam_step).astype(jnp.bfloat16)
    held = merged
    for groups in (far, middle, near):
        held = exchanged(copies(held, len(groups[0])), groups)
    tables = [np.arange(ny * nx * nz).reshape(split).transpose(o).reshape(-1) for o in ORDERS]
    places = jnp.where(core == 0, *(jnp.asarray(t, jnp.int32) for t in tables))
    gathered = placed(held.reshape(-1, rows, width), places).reshape(-1, width)
    return (gathered[None], global_new, momentum_new[None], first_new[None], second_new[None])


def solution(mesh):
    torus = Mesh(
        mesh.devices.reshape(mesh.shape["replica"] // 2, 2, 8, 4, 4), REPLICA + DP
    )
    in_specs = (
        P(REPLICA, DP, None),
        P(REPLICA, DP, None),
        P(REPLICA, DP, None),
        P(DP, None),
        P(DP, REPLICA, None),
        P(REPLICA, DP, None),
        P(REPLICA, DP, None),
    )
    out_specs = (
        P(REPLICA, None, None),
        P(DP, None),
        P(DP, REPLICA, None),
        P(REPLICA, DP, None),
        P(REPLICA, DP, None),
    )
    return jax.shard_map(
        per_device, mesh=torus, in_specs=in_specs, out_specs=out_specs, check_vma=False
    )
```
